32 devices in a mesh: layers: 2 (over y), tok: 4 (over z), feat: 4 (over x, core).
Axes of the slice: x: 2, y: 2, z: 4, core: 2. Of those that a mesh axis runs over, the one named last changes fastest.
Arguments:
- tokens: bfloat16 [4096, 16384], P(('layers', 'tok'), 'feat'), parts along dimension 0, may hold values from -24 to 24
- sketch: bfloat16 [512, 16384], P(None, 'feat'), may hold values from -0.001953125 to 0.001953125
- start: bfloat16 [32, 16384], P(None, 'feat'), may hold values from -8 to 8
Outputs:
- basis: float32 [192, 16384], P('layers', 'feat'), parts along dimension 0
- projected: float32 [192, 64], P('layers'), parts along dimension 0
The draws below stay inside these ranges and needn't reach their ends.
There are 2 independent parts, one for each index of `layers`. The reference program is written for one: setup_inputs(seed, part) draws one part's arguments, and reference() takes and returns one part's arrays. A program takes and returns all parts, laid end to end along the dimension named above; an argument that names none is the same for every part. Nothing has to cross between parts.
All inputs are finite; a program needn't handle non-finite values.
Results may differ from the reference program's by a relative error of at most 0.008.
Values sent between devices are 32-bit elements; how exact they have to be, the bound alone decides.
A program may use at most 64 MiB of HBM per device.

```python
import math
import jax
import jax.numpy as jnp
from jax import lax

D = 16384
B = 32
K = 512
ITERS = 2
TOKENS = 2048


def draw_tokens(key, part):
    key = jax.random.fold_in(key, 11)
    first, second = jax.random.split(key, 2)
    column = jnp.exp(jax.random.uniform(second, (1, D), jnp.float32, math.log(0.4), math.log(4.0)))
    value = jnp.clip(jax.random.normal(first, (TOKENS, D), jnp.float32), -6.0, 6.0) * column
    return jnp.clip(value, -24.0, 24.0).astype(jnp.bfloat16)


def draw_start(key, part):
    key = jax.random.fold_in(key, 23)
    first, second, third = jax.random.split(key, 3)
    own = jnp.clip(jax.random.normal(first, (B, D), jnp.float32), -4.0, 4.0)
    common = jnp.clip(jax.random.normal(second, (1, D), jnp.float32), -4.0, 4.0)
    weight = jax.random.uniform(third, (B, 1), jnp.float32, 0.5, 1.5)
    return jnp.clip(own + weight * common, -8.0, 8.0).astype(jnp.bfloat16)


def steps_of(key, extent, shards, least, high):
    def one(dim, blocks):
        steps = jax.random.uniform(jax.random.fold_in(jax.random.fold_in(key, 6), dim), (blocks,), jnp.float32, least / len(shards), high / len(shards))
        return jnp.repeat(jnp.exp(steps), extent[dim] // blocks).reshape((-1,) + (1,) * (len(extent) - dim - 1))

    gain = one(*shards[0])
    for cut in shards[1:]:
        gain = gain * one(*cut)
    return gain


def normal_values(key, dims, deviation, limit, shards=(), dtype=jnp.bfloat16):
    values = deviation * jax.random.normal(key, dims, jnp.float32)
    if shards:
        values = values * steps_of(key, dims, shards, -0.22, 0.18)
    return jnp.clip(values, -limit, limit).astype(dtype)


def setup_inputs(seed: int = 0, part: int = 0) -> dict:
    arg_keys = jax.random.split(jax.random.key(seed), 4)
    own_keys = jax.random.split(jax.random.fold_in(arg_keys[3], part), 4)
    return {
        "tokens": draw_tokens(jax.random.fold_in(jax.random.fold_in(arg_keys[3], part), 71), part),
        "sketch": normal_values(arg_keys[1], (K, D), (K * D) ** -0.5, 0.001953125, ((1, 4),)),
        "start": draw_start(jax.random.fold_in(arg_keys[3], 71), part),
    }


def orth_block(rows, sketched):
    gram = jnp.dot(sketched, sketched.T, precision=lax.Precision.HIGHEST)
    lower = jnp.linalg.cholesky(gram)
    new_rows = jax.scipy.linalg.solve_triangular(lower, rows, lower=True)
    new_sketched = jax.scipy.linalg.solve_triangular(lower, sketched, lower=True)
    return (new_rows, new_sketched, lower)

def project_coeffs(basis_sk, image_sk):
    return jnp.dot(basis_sk, image_sk.T, precision=lax.Precision.HIGHEST)

def reference(tokens, sketch, start):
    first = start.astype(jnp.float32)
    sketched = jnp.dot(first, sketch.astype(jnp.float32).T, precision=lax.Precision.HIGHEST)
    block, block_sk, lower = orth_block(first, sketched)
    blocks = [block]
    sketches = [block_sk]
    columns = []
    total = (ITERS + 1) * B
    for step in range(ITERS):
        half = block.astype(jnp.bfloat16)
        rows_t = (jnp.dot(half.astype(jnp.float32), tokens.T.astype(jnp.float32), preferred_element_type=jnp.float32) / TOKENS).astype(jnp.bfloat16)
        image = jnp.dot(rows_t.astype(jnp.float32), tokens.astype(jnp.float32), preferred_element_type=jnp.float32)
        image_sk = jnp.dot(image, sketch.astype(jnp.float32).T, precision=lax.Precision.HIGHEST)
        basis = jnp.concatenate(blocks, 0)
        basis_sk = jnp.concatenate(sketches, 0)
        coeffs = project_coeffs(basis_sk, image_sk)
        resid = image - jnp.dot(coeffs.T, basis, precision=lax.Precision.HIGHEST)
        resid_sk = image_sk - jnp.dot(coeffs.T, basis_sk, precision=lax.Precision.HIGHEST)
        block, block_sk, lower = orth_block(resid, resid_sk)
        blocks.append(block)
        sketches.append(block_sk)
        filled = coeffs.shape[0]
        column = jnp.concatenate([coeffs, lower.T, jnp.zeros((total - filled - B, B), jnp.float32)], 0)
        columns.append(column)
    return (jnp.concatenate(blocks, 0), jnp.concatenate(columns, 1))
```

```python
import functools

import jax
import jax.numpy as jnp
from jax import lax
from jax.experimental import pallas as pl
from jax.experimental.pallas import tpu as pltpu
from jax.sharding import PartitionSpec as P

B = 32
ITERS = 2
LAG = 2
MESH = pl.DeviceIdType.MESH
EXACT = lax.Precision.HIGHEST
F32 = jnp.float32
BF16 = jnp.bfloat16


def dot_nn(a, b, precision=None):
    return jnp.dot(a, b, precision=precision, preferred_element_type=F32)


def dot_nt(a, b, precision=None):
    return lax.dot_general(
        a, b, (((1,), (1,)), ((), ())), precision=precision, preferred_element_type=F32
    )


def dot_tn(a, b, precision=None):
    return lax.dot_general(
        a, b, (((0,), (0,)), ((), ())), precision=precision, preferred_element_type=F32
    )


def halves(x):
    hi = x.astype(BF16)
    return hi, (x - hi.astype(F32)).astype(BF16)


def factor(gram):
    n = gram.shape[0]
    row = lax.broadcasted_iota(jnp.int32, (n, n), 0)
    col = lax.broadcasted_iota(jnp.int32, (n, n), 1)
    below = lax.broadcasted_iota(jnp.int32, (n, 1), 0)
    left, right = gram, jnp.where(row == col, 1.0, 0.0).astype(F32)
    for k in range(n - 1):
        inv = 1.0 / left[k : k + 1, k : k + 1]
        mult = jnp.where(below > k, left[:, k : k + 1], 0.0)
        left, right = (
            left - mult * (left[k : k + 1, :] * inv),
            right - mult * (right[k : k + 1, :] * inv),
        )
    diag = jnp.sum(jnp.where(row == col, left, 0.0), axis=1, keepdims=True)
    scale = 1.0 / jnp.sqrt(diag)
    return jnp.where(col >= row, left * scale, 0.0), right * scale


def kernel(
    tsize, fsize, tokens, sketch, start, basis, projected,
    tok, sk, st, sketched_tok, own, rbuf, sbuf, xbuf, stack, yv, zacc, kept, small,
    load_sem, chain_send, chain_recv, ex_send, ex_recv, out_sem,
):
    chunks, rows, width = tok.shape
    t, f = lax.axis_index("tok"), lax.axis_index("feat")
    scale = 1.0 / (rows * tsize)

    barrier = pltpu.get_barrier_semaphore()
    for d in range(1, fsize):
        pl.semaphore_signal(
            barrier, inc=1, device_id={"feat": lax.rem(f + d, fsize)}, device_id_type=MESH
        )

    @pl.when(t > 0)
    def _():
        pl.semaphore_signal(barrier, inc=1, device_id={"tok": t - 1}, device_id_type=MESH)

    @pl.when(t < tsize - 1)
    def _():
        pl.semaphore_signal(barrier, inc=1, device_id={"tok": t + 1}, device_id_type=MESH)

    def load(kind, c):
        cols = pl.ds(c * width, width)
        src, dst = ((start, st), (sketch, sk), (tokens, tok))[kind]
        return pltpu.make_async_copy(src.at[:, cols], dst.at[c], load_sem.at[kind, c])

    for c in range(chunks):
        load(0, c).start()
        load(1, c).start()
    for c in range(chunks):
        load(2, c).start()

    def exchange(phase, slot, peer):
        return pltpu.make_async_remote_copy(
            src_ref=xbuf.at[phase, slot],
            dst_ref=xbuf.at[phase, slot],
            send_sem=ex_send.at[phase, peer],
            recv_sem=ex_recv.at[phase, slot],
            device_id={"feat": peer},
            device_id_type=MESH,
        )

    def spread(phase, value):
        xbuf[phase, f] = value
        for d in range(1, fsize):
            exchange(phase, f, lax.rem(f + d, fsize)).start()

    def collect(phase):
        for d in range(1, fsize):
            peer = lax.rem(f + d, fsize)
            exchange(phase, peer, peer).wait_recv()
        total = xbuf[phase, 0]
        for k in range(1, fsize):
            total = total + xbuf[phase, k]
        return total

    part = jnp.zeros((B, width), F32)
    for c in range(chunks):
        load(0, c).wait()
        load(1, c).wait()
        part = part + dot_nt(st[c], sk[c])

    beside = jnp.where(t > 0, 1, 0) + jnp.where(t < tsize - 1, 1, 0)
    pl.semaphore_wait(barrier, fsize - 1 + beside)

    spread(0, part)
    part = jnp.zeros((B, rows), F32)
    for c in range(chunks):
        load(2, c).wait()
        part = part + dot_nt(st[c], tok[c])
    spread(1, part)

    def sketch_tokens(c, _):
        @pl.when(c == 0)
        def _():
            own_t[...] = dot_nt(tok[c], sk[c])

        @pl.when(c > 0)
        def _():
            own_t[...] += dot_nt(tok[c], sk[c])

        return 0

    own_t = sketched_tok
    lax.fori_loop(0, chunks, sketch_tokens, 0)

    def chain(step, way, slot):
        ahead = t + 1 if way == 0 else t - 1
        src = sbuf.at[step, way, slot]
        return pltpu.make_async_remote_copy(
            src_ref=src,
            dst_ref=rbuf.at[step, way, slot],
            send_sem=chain_send.at[step, way, slot],
            recv_sem=chain_recv.at[step, way, slot],
            device_id={"tok": ahead},
            device_id_type=MESH,
        )

    p_sum = collect(0)
    upper, linv = factor(dot_nt(p_sum, p_sum, EXACT))
    kept[0] = dot_nn(linv, p_sum, EXACT)
    small[0] = linv
    u_sum = collect(1)
    u_now = dot_nn(linv, u_sum, EXACT)
    zacc[1] = u_now
    yv[...] = (u_now * scale).astype(BF16)

    def pipeline(step):
        t_hi, t_lo = halves(sketched_tok[...])
        own[0] = dot_nn(yv[...], t_hi) + dot_nn(yv[...], t_lo)
        if step == 0:
            zacc[0] = jnp.zeros((B, rows), F32)
        lag_r = t * LAG
        lag_l = (tsize - 1 - t) * LAG
        lag_m = jnp.maximum(lag_r, lag_l)

        def body(i, _):
            @pl.when(jnp.logical_and(i >= 1, i <= chunks))
            def _():
                own[i] = dot_nn(yv[...], tok[i - 1])

            for way, lag, first, last in (
                (0, lag_r, t == 0, t == tsize - 1),
                (1, lag_l, t == tsize - 1, t == 0),
            ):
                slot = i - lag

                @pl.when(jnp.logical_and(slot >= 0, slot <= chunks))
                def _():
                    @pl.when(first)
                    def _():
                        sbuf[step, way, slot] = own[slot]
                        chain(step, way, slot).start()

                    @pl.when(jnp.logical_not(first))
                    def _():
                        chain(step, way, slot).wait_recv()

                        @pl.when(jnp.logical_not(last))
                        def _():
                            sbuf[step, way, slot] = own[slot] + rbuf[step, way, slot]
                            chain(step, way, slot).start()

            done = i - lag_m

            @pl.when(jnp.logical_and(done >= 0, done <= chunks))
            def _():
                @pl.when(t == 0)
                def _():
                    own[done] = own[done] + rbuf[step, 1, done]

                @pl.when(t == tsize - 1)
                def _():
                    own[done] = own[done] + rbuf[step, 0, done]

                @pl.when(jnp.logical_and(t > 0, t < tsize - 1))
                def _():
                    own[done] = own[done] + rbuf[step, 0, done] + rbuf[step, 1, done]

                @pl.when(done == 0)
                def _():
                    spread(2 + 2 * step, own[0])

                @pl.when(done > 0)
                def _():
                    c = done - 1
                    image = own[done]
                    if step == 0:
                        stack[c, 2 * B :, :] = image
                        hi, lo = halves(image)
                        zacc[0] += dot_nt(hi, tok[c]) + dot_nt(lo, tok[c])
                        stack[c, :B, :] = dot_nn(small[0], st[c].astype(F32), EXACT)
                    else:
                        block = dot_nn(small[1], stack[c, :B, :], EXACT) + dot_nn(
                            small[2], stack[c, 2 * B :, :], EXACT
                        )
                        stack[c, B : 2 * B, :] = block
                        stack[c, 2 * B :, :] = image

            return 0

        lax.fori_loop(0, chunks + 1 + LAG * (tsize - 1), body, 0)

    pipeline(0)
    spread(3, zacc[0])
    image_sk = collect(2)
    coeffs = dot_nt(kept[0], image_sk, EXACT)
    resid_sk = image_sk - dot_tn(coeffs, kept[0], EXACT)
    upper, linv = factor(dot_nt(resid_sk, resid_sk, EXACT))
    kept[1] = dot_nn(linv, resid_sk, EXACT)
    small[1] = -dot_nt(linv, coeffs, EXACT)
    small[2] = linv
    projected[:B, :B] = coeffs
    projected[B : 2 * B, :B] = upper
    projected[2 * B :, :B] = jnp.zeros((B, B), F32)
    z_sum = collect(3)
    yv[...] = (
        dot_nn(linv, z_sum - dot_tn(coeffs, zacc[1], EXACT), EXACT) * scale
    ).astype(BF16)

    pipeline(1)
    image_sk = collect(4)
    first_co = dot_nt(kept[0], image_sk, EXACT)
    second_co = dot_nt(kept[1], image_sk, EXACT)
    resid_sk = (
        image_sk - dot_tn(first_co, kept[0], EXACT) - dot_tn(second_co, kept[1], EXACT)
    )
    upper, linv = factor(dot_nt(resid_sk, resid_sk, EXACT))
    projected[:B, B:] = first_co
    projected[B : 2 * B, B:] = second_co
    projected[2 * B :, B:] = upper
    small[0] = -dot_nt(linv, first_co, EXACT)
    small[1] = -dot_nt(linv, second_co, EXACT)
    small[2] = linv

    def write(c):
        return pltpu.make_async_copy(
            stack.at[c],
            basis.at[:, pl.ds(pl.multiple_of(c * width, width), width)],
            out_sem.at[c],
        )

    for c in range(chunks):
        block = dot_nn(small[0], stack[c, :B, :], EXACT)
        block += dot_nn(small[1], stack[c, B : 2 * B, :], EXACT)
        block += dot_nn(small[2], stack[c, 2 * B :, :], EXACT)
        stack[c, 2 * B :, :] = block
        write(c).start()

    for phase in range(1 + 2 * ITERS):
        for d in range(1, fsize):
            exchange(phase, f, lax.rem(f + d, fsize)).wait_send()

    def drain(slot, _):
        for step in range(ITERS):

            @pl.when(t < tsize - 1)
            def _():
                chain(step, 0, slot).wait_send()

            @pl.when(t > 0)
            def _():
                chain(step, 1, slot).wait_send()

        return 0

    lax.fori_loop(0, chunks + 1, drain, 0)
    for c in range(chunks):
        write(c).wait()


def per_device(tsize, fsize, tokens, sketch, start):
    rows, features = tokens.shape
    width = sketch.shape[0]
    chunks = features // width
    total = (ITERS + 1) * B
    any_spec = pl.BlockSpec(memory_space=pl.ANY)
    return pl.pallas_call(
        functools.partial(kernel, tsize, fsize),
        out_shape=(
            jax.ShapeDtypeStruct((total, features), F32),
            jax.ShapeDtypeStruct((total, ITERS * B), F32),
        ),
        in_specs=[any_spec] * 3,
        out_specs=(any_spec, pl.BlockSpec(memory_space=pltpu.VMEM)),
        scratch_shapes=[
            pltpu.VMEM((chunks, rows, width), BF16),
            pltpu.VMEM((chunks, width, width), BF16),
            pltpu.VMEM((chunks, B, width), BF16),
            pltpu.VMEM((rows, width), F32),
            pltpu.VMEM((chunks + 1, B, width), F32),
            pltpu.VMEM((ITERS, 2, chunks + 1, B, width), F32),
            pltpu.VMEM((ITERS, 2, chunks + 1, B, width), F32),
            pltpu.VMEM((1 + 2 * ITERS, fsize, B, width), F32),
            pltpu.VMEM((chunks, total, width), F32),
            pltpu.VMEM((B, rows), BF16),
            pltpu.VMEM((2, B, rows), F32),
            pltpu.VMEM((2, B, width), F32),
            pltpu.VMEM((3, B, B), F32),
            pltpu.SemaphoreType.DMA((3, chunks)),
            pltpu.SemaphoreType.DMA((ITERS, 2, chunks + 1)),
            pltpu.SemaphoreType.DMA((ITERS, 2, chunks + 1)),
            pltpu.SemaphoreType.DMA((1 + 2 * ITERS, fsize)),
            pltpu.SemaphoreType.DMA((1 + 2 * ITERS, fsize)),
            pltpu.SemaphoreType.DMA((chunks,)),
        ],
        compiler_params=pltpu.CompilerParams(
            collective_id=0, has_side_effects=True, vmem_limit_bytes=48 * 1024 * 1024
        ),
    )(tokens, sketch, start)


def solution(mesh):
    placed = (P(("layers", "tok"), "feat"), P(None, "feat"), P(None, "feat"))
    return jax.shard_map(
        functools.partial(per_device, mesh.shape["tok"], mesh.shape["feat"]),
        mesh=mesh,
        in_specs=placed,
        out_specs=(P("layers", "feat"), P("layers", None)),
        check_vma=False,
    )
```

```python
import functools

import jax
import jax.numpy as jnp
from jax import lax
from jax.experimental import pallas as pl
from jax.experimental.pallas import tpu as pltpu
from jax.sharding import PartitionSpec as P

B = 32
ITERS = 2
LAG = 3
WAIT = 3
STAGES = 5
MESH = pl.DeviceIdType.MESH
EXACT = lax.Precision.HIGHEST
F32 = jnp.float32
BF16 = jnp.bfloat16


def dot_nn(a, b, precision=None):
    return jnp.dot(a, b, precision=precision, preferred_element_type=F32)


def dot_nt(a, b, precision=None):
    return lax.dot_general(
        a, b, (((1,), (1,)), ((), ())), precision=precision, preferred_element_type=F32
    )


def dot_tn(a, b, precision=None):
    return lax.dot_general(
        a, b, (((0,), (0,)), ((), ())), precision=precision, preferred_element_type=F32
    )


def halves(x):
    hi = x.astype(BF16)
    return hi, (x - hi.astype(F32)).astype(BF16)


def grid_iota(n):
    return (
        lax.broadcasted_iota(jnp.int32, (n, n), 0),
        lax.broadcasted_iota(jnp.int32, (n, n), 1),
    )


def eliminate(left, right, first, last):
    below = lax.broadcasted_iota(jnp.int32, (left.shape[0], 1), 0)
    for k in range(first, last):
        inv = 1.0 / left[k : k + 1, k : k + 1]
        mult = jnp.where(below > k, left[:, k : k + 1], 0.0)
        left, right = (
            left - mult * (left[k : k + 1, :] * inv),
            right - mult * (right[k : k + 1, :] * inv),
        )
    return left, right


def identity(n):
    row, col = grid_iota(n)
    return jnp.where(row == col, 1.0, 0.0).astype(F32)


def finish(left, right):
    row, col = grid_iota(left.shape[0])
    diag = jnp.sum(jnp.where(row == col, left, 0.0), axis=1, keepdims=True)
    scale = 1.0 / jnp.sqrt(diag)
    return jnp.where(col >= row, left * scale, 0.0), right * scale


def kernel(
    tsize, fsize, tokens, sketch, start, basis, projected,
    tok, sk, st, sketched_tok, own, rbuf, sbuf, xbuf, stack, yv, zacc, kept, small, work, cof,
    load_sem, chain_send, chain_recv, ex_send, ex_recv, out_sem,
):
    chunks, rows, width = tok.shape
    t, f = lax.axis_index("tok"), lax.axis_index("feat")
    scale = 1.0 / (rows * tsize)

    barrier = pltpu.get_barrier_semaphore()
    for d in range(1, fsize):
        pl.semaphore_signal(
            barrier, inc=1, device_id={"feat": lax.rem(f + d, fsize)}, device_id_type=MESH
        )

    @pl.when(t > 0)
    def _():
        pl.semaphore_signal(barrier, inc=1, device_id={"tok": t - 1}, device_id_type=MESH)

    @pl.when(t < tsize - 1)
    def _():
        pl.semaphore_signal(barrier, inc=1, device_id={"tok": t + 1}, device_id_type=MESH)

    def load(kind, c):
        cols = pl.ds(c * width, width)
        src, dst = ((start, st), (sketch, sk), (tokens, tok))[kind]
        return pltpu.make_async_copy(src.at[:, cols], dst.at[c], load_sem.at[kind, c])

    for c in range(chunks):
        load(0, c).start()
        load(1, c).start()
    for c in range(chunks):
        load(2, c).start()

    def exchange(phase, slot, peer):
        return pltpu.make_async_remote_copy(
            src_ref=xbuf.at[phase, slot],
            dst_ref=xbuf.at[phase, slot],
            send_sem=ex_send.at[phase, peer],
            recv_sem=ex_recv.at[phase, slot],
            device_id={"feat": peer},
            device_id_type=MESH,
        )

    def spread(phase, value):
        xbuf[phase, f] = value
        for d in range(1, fsize):
            exchange(phase, f, lax.rem(f + d, fsize)).start()

    def collect(phase):
        for d in range(1, fsize):
            peer = lax.rem(f + d, fsize)
            exchange(phase, peer, peer).wait_recv()
        total = xbuf[phase, 0]
        for k in range(1, fsize):
            total = total + xbuf[phase, k]
        return total

    part = jnp.zeros((B, width), F32)
    for c in range(chunks):
        load(0, c).wait()
        load(1, c).wait()
        part = part + dot_nt(st[c], sk[c])

    beside = jnp.where(t > 0, 1, 0) + jnp.where(t < tsize - 1, 1, 0)
    pl.semaphore_wait(barrier, fsize - 1 + beside)

    spread(0, part)
    part = jnp.zeros((B, rows), F32)
    for c in range(chunks):
        load(2, c).wait()
        part = part + dot_nt(st[c], tok[c])
    spread(1, part)

    def sketch_tokens(c, _):
        @pl.when(c == 0)
        def _():
            own_t[...] = dot_nt(tok[c], sk[c])

        @pl.when(c > 0)
        def _():
            own_t[...] += dot_nt(tok[c], sk[c])

        return 0

    own_t = sketched_tok
    lax.fori_loop(0, chunks, sketch_tokens, 0)

    def chain(step, way, slot):
        ahead = t + 1 if way == 0 else t - 1
        src = sbuf.at[step, way, slot]
        return pltpu.make_async_remote_copy(
            src_ref=src,
            dst_ref=rbuf.at[step, way, slot],
            send_sem=chain_send.at[step, way, slot],
            recv_sem=chain_recv.at[step, way, slot],
            device_id={"tok": ahead},
            device_id_type=MESH,
        )

    p_sum = collect(0)
    upper, linv = finish(*eliminate(dot_nt(p_sum, p_sum, EXACT), identity(B), 0, B - 1))
    kept[0] = dot_nn(linv, p_sum, EXACT)
    small[0] = linv
    u_sum = collect(1)
    u_now = dot_nn(linv, u_sum, EXACT)
    zacc[1] = u_now
    yv[...] = (u_now * scale).astype(BF16)

    def advance(step, stage):
        if stage == 0:
            image_sk = collect(2 + 2 * step)
            kept[2] = image_sk
            for j in range(step + 1):
                cof[j] = dot_nt(kept[j], image_sk, EXACT)
        elif stage == 1:
            resid_sk = kept[2]
            for j in range(step + 1):
                resid_sk = resid_sk - dot_tn(cof[j], kept[j], EXACT)
            kept[2] = resid_sk
        elif stage == 2:
            resid_sk = kept[2]
            gram = dot_nt(resid_sk, resid_sk, EXACT)
            work[0], work[1] = eliminate(gram, identity(B), 0, 8)
        elif stage == 3:
            work[0], work[1] = eliminate(work[0], work[1], 8, 20)
        else:
            upper, linv = finish(*eliminate(work[0], work[1], 20, B - 1))
            place = slice(step * B, (step + 1) * B)
            for j in range(step + 1):
                projected[j * B : (j + 1) * B, place] = cof[j]
                small[1 + 2 * step + j] = -dot_nt(linv, cof[j], EXACT)
            projected[(step + 1) * B : (step + 2) * B, place] = upper
            small[2 + 3 * step] = linv
            if step == 0:
                projected[2 * B :, place] = jnp.zeros((B, B), F32)
                kept[1] = dot_nn(linv, kept[2], EXACT)
                zacc[1] = dot_nn(small[1], zacc[1], EXACT)

    def pipeline(step):
        t_hi, t_lo = halves(sketched_tok[...])
        own[0] = dot_nn(yv[...], t_hi) + dot_nn(yv[...], t_lo)
        if step == 0:
            zacc[0] = jnp.zeros((B, rows), F32)
        lag_r = t * LAG
        lag_l = (tsize - 1 - t) * LAG
        lag_m = jnp.maximum(lag_r, lag_l)

        def body(i, _):
            @pl.when(jnp.logical_and(i >= 1, i <= chunks))
            def _():
                own[i] = dot_nn(yv[...], tok[i - 1])

            for way, lag, first, last in (
                (0, lag_r, t == 0, t == tsize - 1),
                (1, lag_l, t == tsize - 1, t == 0),
            ):
                slot = i - lag

                @pl.when(jnp.logical_and(slot >= 0, slot <= chunks))
                def _():
                    @pl.when(first)
                    def _():
                        sbuf[step, way, slot] = own[slot]
                        chain(step, way, slot).start()

                    @pl.when(jnp.logical_not(first))
                    def _():
                        chain(step, way, slot).wait_recv()

                        @pl.when(jnp.logical_not(last))
                        def _():
                            sbuf[step, way, slot] = own[slot] + rbuf[step, way, slot]
                            chain(step, way, slot).start()

            done = i - lag_m

            @pl.when(jnp.logical_and(done >= 0, done <= chunks))
            def _():
                @pl.when(t == 0)
                def _():
                    own[done] = own[done] + rbuf[step, 1, done]

                @pl.when(t == tsize - 1)
                def _():
                    own[done] = own[done] + rbuf[step, 0, done]

                @pl.when(jnp.logical_and(t > 0, t < tsize - 1))
                def _():
                    own[done] = own[done] + rbuf[step, 0, done] + rbuf[step, 1, done]

                @pl.when(done == 0)
                def _():
                    spread(2 + 2 * step, own[0])

                @pl.when(done > 0)
                def _():
                    c = done - 1
                    image = own[done]
                    if step == 0:
                        stack[c, 2 * B :, :] = image
                        hi, lo = halves(image)
                        zacc[0] += dot_nt(hi, tok[c]) + dot_nt(lo, tok[c])
                        stack[c, :B, :] = dot_nn(small[0], st[c].astype(F32), EXACT)
                    else:
                        block = dot_nn(small[1], stack[c, :B, :], EXACT) + dot_nn(
                            small[2], stack[c, 2 * B :, :], EXACT
                        )
                        stack[c, B : 2 * B, :] = block
                        stack[c, 2 * B :, :] = image

            for stage in range(STAGES):

                @pl.when(i == lag_m + WAIT + stage)
                def _():
                    advance(step, stage)

            return 0

        turns = max(chunks + 1, WAIT + STAGES) + LAG * (tsize - 1)
        lax.fori_loop(0, turns, body, 0)

    pipeline(0)
    spread(3, zacc[0])
    z_sum = collect(3)
    yv[...] = ((dot_nn(small[2], z_sum, EXACT) + zacc[1]) * scale).astype(BF16)

    pipeline(1)
    last = jnp.concatenate([small[3], small[4], small[5]], 1)

    def write(c):
        return pltpu.make_async_copy(
            stack.at[c],
            basis.at[:, pl.ds(pl.multiple_of(c * width, width), width)],
            out_sem.at[c],
        )

    for c in range(chunks):
        block = dot_nn(last, stack[c], EXACT)
        stack[c, 2 * B :, :] = block
        write(c).start()

    for phase in range(1 + 2 * ITERS):
        for d in range(1, fsize):
            exchange(phase, f, lax.rem(f + d, fsize)).wait_send()

    def drain(slot, _):
        for step in range(ITERS):

            @pl.when(t < tsize - 1)
            def _():
                chain(step, 0, slot).wait_send()

            @pl.when(t > 0)
            def _():
                chain(step, 1, slot).wait_send()

        return 0

    lax.fori_loop(0, chunks + 1, drain, 0)
    for c in range(chunks):
        write(c).wait()


def per_device(tsize, fsize, tokens, sketch, start):
    rows, features = tokens.shape
    width = sketch.shape[0]
    chunks = features // width
    total = (ITERS + 1) * B
    any_spec = pl.BlockSpec(memory_space=pl.ANY)
    return pl.pallas_call(
        functools.partial(kernel, tsize, fsize),
        out_shape=(
            jax.ShapeDtypeStruct((total, features), F32),
            jax.ShapeDtypeStruct((total, ITERS * B), F32),
        ),
        in_specs=[any_spec] * 3,
        out_specs=(any_spec, pl.BlockSpec(memory_space=pltpu.VMEM)),
        scratch_shapes=[
            pltpu.VMEM((chunks, rows, width), BF16),
            pltpu.VMEM((chunks, width, width), BF16),
            pltpu.VMEM((chunks, B, width), BF16),
            pltpu.VMEM((rows, width), F32),
            pltpu.VMEM((chunks + 1, B, width), F32),
            pltpu.VMEM((ITERS, 2, chunks + 1, B, width), F32),
            pltpu.VMEM((ITERS, 2, chunks + 1, B, width), F32),
            pltpu.VMEM((1 + 2 * ITERS, fsize, B, width), F32),
            pltpu.VMEM((chunks, total, width), F32),
            pltpu.VMEM((B, rows), BF16),
            pltpu.VMEM((2, B, rows), F32),
            pltpu.VMEM((3, B, width), F32),
            pltpu.VMEM((6, B, B), F32),
            pltpu.VMEM((2, B, B), F32),
            pltpu.VMEM((ITERS, B, B), F32),
            pltpu.SemaphoreType.DMA((3, chunks)),
            pltpu.SemaphoreType.DMA((ITERS, 2, chunks + 1)),
            pltpu.SemaphoreType.DMA((ITERS, 2, chunks + 1)),
            pltpu.SemaphoreType.DMA((1 + 2 * ITERS, fsize)),
            pltpu.SemaphoreType.DMA((1 + 2 * ITERS, fsize)),
            pltpu.SemaphoreType.DMA((chunks,)),
        ],
        compiler_params=pltpu.CompilerParams(
            collective_id=0, has_side_effects=True, vmem_limit_bytes=60 * 1024 * 1024
        ),
    )(tokens, sketch, start)


def solution(mesh):
    placed = (P(("layers", "tok"), "feat"), P(None, "feat"), P(None, "feat"))
    return jax.shard_map(
        functools.partial(per_device, mesh.shape["tok"], mesh.shape["feat"]),
        mesh=mesh,
        in_specs=placed,
        out_specs=(P("layers", "feat"), P("layers", None)),
        check_vma=False,
    )
```

```python
import functools

import jax
import jax.numpy as jnp
from jax import lax
from jax.experimental import pallas as pl
from jax.experimental.pallas import tpu as pltpu
from jax.sharding import PartitionSpec as P

B = 32
ITERS = 2
LAG = 3
WAIT = 3
STAGES = 5
MESH = pl.DeviceIdType.MESH
EXACT = lax.Precision.HIGHEST
F32 = jnp.float32
BF16 = jnp.bfloat16


def dot_nn(a, b, precision=None):
    return jnp.dot(a, b, precision=precision, preferred_element_type=F32)


def dot_nt(a, b, precision=None):
    return lax.dot_general(
        a, b, (((1,), (1,)), ((), ())), precision=precision, preferred_element_type=F32
    )


def halves(x):
    hi = x.astype(BF16)
    return hi, (x - hi.astype(F32)).astype(BF16)


def grid_iota(n):
    return (
        lax.broadcasted_iota(jnp.int32, (n, n), 0),
        lax.broadcasted_iota(jnp.int32, (n, n), 1),
    )


def eliminate(left, right, first, last):
    below = lax.broadcasted_iota(jnp.int32, (left.shape[0], 1), 0)
    for k in range(first, last):
        inv = 1.0 / left[k : k + 1, k : k + 1]
        mult = jnp.where(below > k, left[:, k : k + 1], 0.0)
        left, right = (
            left - mult * (left[k : k + 1, :] * inv),
            right - mult * (right[k : k + 1, :] * inv),
        )
    return left, right


def identity(n):
    row, col = grid_iota(n)
    return jnp.where(row == col, 1.0, 0.0).astype(F32)


def finish(left, right):
    row, col = grid_iota(left.shape[0])
    diag = jnp.sum(jnp.where(row == col, left, 0.0), axis=1, keepdims=True)
    scale = 1.0 / jnp.sqrt(diag)
    return jnp.where(col >= row, left * scale, 0.0), right * scale


def kernel(
    tsize, fsize, tokens, sketch, start, basis, projected,
    tok, sk, st, sketched_tok, own, rbuf, sbuf, xbuf, stack, yv, zacc, kept, small, work, cof,
    load_sem, chain_send, chain_recv, ex_send, ex_recv, out_sem,
):
    chunks, rows, width = tok.shape
    t, f = lax.axis_index("tok"), lax.axis_index("feat")
    scale = 1.0 / (rows * tsize)

    barrier = pltpu.get_barrier_semaphore()
    for d in range(1, fsize):
        pl.semaphore_signal(
            barrier, inc=1, device_id={"feat": lax.rem(f + d, fsize)}, device_id_type=MESH
        )

    @pl.when(t > 0)
    def _():
        pl.semaphore_signal(barrier, inc=1, device_id={"tok": t - 1}, device_id_type=MESH)

    @pl.when(t < tsize - 1)
    def _():
        pl.semaphore_signal(barrier, inc=1, device_id={"tok": t + 1}, device_id_type=MESH)

    def load(kind, c):
        cols = pl.ds(c * width, width)
        src, dst = ((start, st), (sketch, sk), (tokens, tok))[kind]
        return pltpu.make_async_copy(src.at[:, cols], dst.at[c], load_sem.at[kind, c])

    for c in range(chunks):
        load(0, c).start()
        load(1, c).start()
    for c in range(chunks):
        load(2, c).start()

    def exchange(phase, slot, peer):
        return pltpu.make_async_remote_copy(
            src_ref=xbuf.at[phase, slot],
            dst_ref=xbuf.at[phase, slot],
            send_sem=ex_send.at[phase, peer],
            recv_sem=ex_recv.at[phase, slot],
            device_id={"feat": peer},
            device_id_type=MESH,
        )

    def spread(phase, value):
        xbuf[phase, f] = value
        for d in range(1, fsize):
            exchange(phase, f, lax.rem(f + d, fsize)).start()

    def collect(phase):
        for d in range(1, fsize):
            peer = lax.rem(f + d, fsize)
            exchange(phase, peer, peer).wait_recv()
        total = xbuf[phase, 0]
        for k in range(1, fsize):
            total = total + xbuf[phase, k]
        return total

    part = jnp.zeros((B, width), F32)
    for c in range(chunks):
        load(0, c).wait()
        load(1, c).wait()
        part = part + dot_nt(st[c], sk[c])

    beside = jnp.where(t > 0, 1, 0) + jnp.where(t < tsize - 1, 1, 0)
    pl.semaphore_wait(barrier, fsize - 1 + beside)

    spread(0, part)
    part = jnp.zeros((B, rows), F32)
    for c in range(chunks):
        load(2, c).wait()
        part = part + dot_nt(st[c], tok[c])
    spread(1, part)

    def sketch_tokens(c, _):
        @pl.when(c == 0)
        def _():
            own_t[...] = dot_nt(tok[c], sk[c])

        @pl.when(c > 0)
        def _():
            own_t[...] += dot_nt(tok[c], sk[c])

        return 0

    own_t = sketched_tok
    lax.fori_loop(0, chunks, sketch_tokens, 0)

    def chain(step, way, slot):
        ahead = t + 1 if way == 0 else t - 1
        src = sbuf.at[step, way, slot]
        return pltpu.make_async_remote_copy(
            src_ref=src,
            dst_ref=rbuf.at[step, way, slot],
            send_sem=chain_send.at[step, way, slot],
            recv_sem=chain_recv.at[step, way, slot],
            device_id={"tok": ahead},
            device_id_type=MESH,
        )

    p_sum = collect(0)
    upper, linv = finish(*eliminate(dot_nt(p_sum, p_sum, EXACT), identity(B), 0, B - 1))
    kept[0] = dot_nn(linv, p_sum, EXACT)
    small[0] = linv
    u_sum = collect(1)
    u_now = dot_nn(linv, u_sum, EXACT)
    zacc[1] = u_now
    yv[...] = (u_now * scale).astype(BF16)

    def advance(step, stage):
        if stage == 0:
            image_sk = collect(2 + 2 * step)
            kept[2] = image_sk
            for j in range(step + 1):
                cof[j] = dot_nt(image_sk, kept[j], EXACT)
        elif stage == 1:
            resid_sk = kept[2]
            for j in range(step + 1):
                resid_sk = resid_sk - dot_nn(cof[j], kept[j], EXACT)
            kept[2] = resid_sk
        elif stage == 2:
            resid_sk = kept[2]
            gram = dot_nt(resid_sk, resid_sk, EXACT)
            work[0], work[1] = eliminate(gram, identity(B), 0, 8)
        elif stage == 3:
            work[0], work[1] = eliminate(work[0], work[1], 8, 20)
        else:
            upper, linv = finish(*eliminate(work[0], work[1], 20, B - 1))
            place = slice(step * B, (step + 1) * B)
            for j in range(step + 1):
                projected[place, j * B : (j + 1) * B] = cof[j]
                small[1 + 2 * step + j] = -dot_nn(linv, cof[j], EXACT)
            projected[place, (step + 1) * B : (step + 2) * B] = dot_nt(identity(B), upper, EXACT)
            small[2 + 3 * step] = linv
            if step == 0:
                projected[place, 2 * B :] = jnp.zeros((B, B), F32)
                kept[1] = dot_nn(linv, kept[2], EXACT)
                zacc[1] = dot_nn(small[1], zacc[1], EXACT)

    def pipeline(step):
        t_hi, t_lo = halves(sketched_tok[...])
        own[0] = dot_nn(yv[...], t_hi) + dot_nn(yv[...], t_lo)
        if step == 0:
            zacc[0] = jnp.zeros((B, rows), F32)
        lag_r = t * LAG
        lag_l = (tsize - 1 - t) * LAG
        lag_m = jnp.maximum(lag_r, lag_l)

        def body(i, _):
            @pl.when(jnp.logical_and(i >= 1, i <= chunks))
            def _():
                own[i] = dot_nn(yv[...], tok[i - 1])

            for way, lag, first, last in (
                (0, lag_r, t == 0, t == tsize - 1),
                (1, lag_l, t == tsize - 1, t == 0),
            ):
                slot = i - lag

                @pl.when(jnp.logical_and(slot >= 0, slot <= chunks))
                def _():
                    @pl.when(first)
                    def _():
                        sbuf[step, way, slot] = own[slot]
                        chain(step, way, slot).start()

                    @pl.when(jnp.logical_not(first))
                    def _():
                        chain(step, way, slot).wait_recv()

                        @pl.when(jnp.logical_not(last))
                        def _():
                            sbuf[step, way, slot] = own[slot] + rbuf[step, way, slot]
                            chain(step, way, slot).start()

            done = i - lag_m

            @pl.when(jnp.logical_and(done >= 0, done <= chunks))
            def _():
                @pl.when(t == 0)
                def _():
                    own[done] = own[done] + rbuf[step, 1, done]

                @pl.when(t == tsize - 1)
                def _():
                    own[done] = own[done] + rbuf[step, 0, done]

                @pl.when(jnp.logical_and(t > 0, t < tsize - 1))
                def _():
                    own[done] = own[done] + rbuf[step, 0, done] + rbuf[step, 1, done]

                @pl.when(done == 0)
                def _():
                    spread(2 + 2 * step, own[0])

                @pl.when(done > 0)
                def _():
                    c = done - 1
                    image = own[done]
                    if step == 0:
                        stack[c, 2 * B :, :] = image
                        hi, lo = halves(image)
                        zacc[0] += dot_nt(hi, tok[c]) + dot_nt(lo, tok[c])
                        stack[c, :B, :] = dot_nn(small[0], st[c].astype(F32), EXACT)
                    else:
                        block = dot_nn(small[1], stack[c, :B, :], EXACT) + dot_nn(
                            small[2], stack[c, 2 * B :, :], EXACT
                        )
                        stack[c, B : 2 * B, :] = block
                        stack[c, 2 * B :, :] = image

            for stage in range(STAGES):

                @pl.when(i == lag_m + WAIT + stage)
                def _():
                    advance(step, stage)

            return 0

        turns = max(chunks + 1, WAIT + STAGES) + LAG * (tsize - 1)
        lax.fori_loop(0, turns, body, 0)

    pipeline(0)
    spread(3, zacc[0])
    z_sum = collect(3)
    yv[...] = ((dot_nn(small[2], z_sum, EXACT) + zacc[1]) * scale).astype(BF16)

    pipeline(1)
    last = jnp.concatenate([small[3], small[4], small[5]], 1)

    def write(c):
        return pltpu.make_async_copy(
            stack.at[c],
            basis.at[:, pl.ds(pl.multiple_of(c * width, width), width)],
            out_sem.at[c],
        )

    for c in range(chunks):
        block = dot_nn(last, stack[c], EXACT)
        stack[c, 2 * B :, :] = block
        write(c).start()

    for phase in range(1 + 2 * ITERS):
        for d in range(1, fsize):
            exchange(phase, f, lax.rem(f + d, fsize)).wait_send()

    def drain(slot, _):
        for step in range(ITERS):

            @pl.when(t < tsize - 1)
            def _():
                chain(step, 0, slot).wait_send()

            @pl.when(t > 0)
            def _():
                chain(step, 1, slot).wait_send()

        return 0

    lax.fori_loop(0, chunks + 1, drain, 0)
    for c in range(chunks):
        write(c).wait()


def per_device(tsize, fsize, tokens, sketch, start):
    rows, features = tokens.shape
    width = sketch.shape[0]
    chunks = features // width
    total = (ITERS + 1) * B
    any_spec = pl.BlockSpec(memory_space=pl.ANY)
    basis, projected = pl.pallas_call(
        functools.partial(kernel, tsize, fsize),
        out_shape=(
            jax.ShapeDtypeStruct((total, features), F32),
            jax.ShapeDtypeStruct((ITERS * B, total), F32),
        ),
        in_specs=[any_spec] * 3,
        out_specs=(any_spec, pl.BlockSpec(memory_space=pltpu.VMEM)),
        scratch_shapes=[
            pltpu.VMEM((chunks, rows, width), BF16),
            pltpu.VMEM((chunks, width, width), BF16),
            pltpu.VMEM((chunks, B, width), BF16),
            pltpu.VMEM((rows, width), F32),
            pltpu.VMEM((chunks + 1, B, width), F32),
            pltpu.VMEM((ITERS, 2, chunks + 1, B, width), F32),
            pltpu.VMEM((ITERS, 2, chunks + 1, B, width), F32),
            pltpu.VMEM((1 + 2 * ITERS, fsize, B, width), F32),
            pltpu.VMEM((chunks, total, width), F32),
            pltpu.VMEM((B, rows), BF16),
            pltpu.VMEM((2, B, rows), F32),
            pltpu.VMEM((3, B, width), F32),
            pltpu.VMEM((6, B, B), F32),
            pltpu.VMEM((2, B, B), F32),
            pltpu.VMEM((ITERS, B, B), F32),
            pltpu.SemaphoreType.DMA((3, chunks)),
            pltpu.SemaphoreType.DMA((ITERS, 2, chunks + 1)),
            pltpu.SemaphoreType.DMA((ITERS, 2, chunks + 1)),
            pltpu.SemaphoreType.DMA((1 + 2 * ITERS, fsize)),
            pltpu.SemaphoreType.DMA((1 + 2 * ITERS, fsize)),
            pltpu.SemaphoreType.DMA((chunks,)),
        ],
        compiler_params=pltpu.CompilerParams(
            collective_id=0, has_side_effects=True, vmem_limit_bytes=60 * 1024 * 1024
        ),
    )(tokens, sketch, start)
    return basis, projected.T


def solution(mesh):
    placed = (P(("layers", "tok"), "feat"), P(None, "feat"), P(None, "feat"))
    return jax.shard_map(
        functools.partial(per_device, mesh.shape["tok"], mesh.shape["feat"]),
        mesh=mesh,
        in_specs=placed,
        out_specs=(P("layers", "feat"), P("layers", None)),
        check_vma=False,
    )
```
